32 devices in a mesh: angle: 4 (over z), tile: 8 (over y, x, core).
Axes of the slice: x: 2, y: 2, z: 4, core: 2. Of those that a mesh axis runs over, the one named last changes fastest.
Arguments:
- object_field: float32 [4, 2, 2048, 256], P('angle', None, 'tile'), may hold values from -6 to 6
- probe: float32 [2, 2, 128, 128], replicated, may hold values from -6 to 6
- amplitudes: float32 [4, 8, 3, 4, 128, 128], P('angle', 'tile'), may hold values from 0.2 to 3
- positions: int32 [4, 8, 3, 4, 2], P('angle', 'tile'), may hold values from 0 to 255, as said below
Outputs:
- object_out: float32 [4, 2, 2048, 256], P('angle', None, 'tile')
- probe_out: float32 [2, 2, 128, 128], replicated
The draws below stay inside these ranges and needn't reach their ends.
Inputs may be any that keep to these rules, and one draw needn't show every extreme that they name: `positions`: the row entry lies in 0 to 255 and takes both ends on every device in every pass; the column entry lies in 0 to 128 and takes both ends on every device in the first pass.
All inputs are finite; a program needn't handle non-finite values.
Results may differ from the reference program's by a relative error of at most 0.0003.
Values sent between devices are 32-bit elements; how exact they have to be, the bound alone decides.
A program may use at most 64 MiB of HBM per device.

```python
import math
import jax
import jax.numpy as jnp
from jax import lax

FRAME = 128
HALF = 64
MODES = 2
ROWS = 256
WIDTH = 256
POS = 4
PASSES = 3
ANGLES = 4
TILES = 8
OBJ_ROWS = 2048


def draw_positions(key, part):
    key = jax.random.fold_in(key, 7)
    key_rows, key_cols = jax.random.split(key)
    shape = (ANGLES, TILES, PASSES, POS)
    rows = jax.random.randint(key_rows, shape, 0, ROWS)
    cols = jax.random.randint(key_cols, shape, 0, WIDTH - FRAME + 1)
    rows = rows.at[..., 0].set(ROWS - 1).at[..., 1].set(0)
    cols = cols.at[:, :, 0, 0].set(WIDTH - FRAME).at[:, :, 0, 1].set(0)
    return jnp.stack([rows, cols], axis=-1).astype(jnp.int32)


def level_of(rng, dims, pieces, low, high):
    gain = 1.0
    for axis_at, parts in pieces:
        draws = jax.random.uniform(jax.random.fold_in(jax.random.fold_in(rng, 6), axis_at), (parts,), jnp.float32, low / len(pieces), high / len(pieces))
        gain = gain * jnp.repeat(jnp.exp(draws), dims[axis_at] // parts).reshape((-1,) + (1,) * (len(dims) - 1 - axis_at))
    return gain


def noise(key, shape, scale, reach, cuts=(), held_as=jnp.bfloat16):
    entries = scale * jax.random.normal(key, shape, jnp.float32)
    if cuts:
        entries = entries * level_of(key, shape, cuts, -0.22, 0.18)
    return jnp.clip(entries, -reach, reach).astype(held_as)


def setup_inputs(seed: int = 0) -> dict:
    seeds = jax.random.split(jax.random.key(seed), 5)
    object_field = noise(seeds[0], (ANGLES, 2, OBJ_ROWS, WIDTH), 1.0, 6.0, ((0, 4), (2, 8)), jnp.float32)
    probe = noise(seeds[1], (2, MODES, FRAME, FRAME), 1.0, 6.0, (), jnp.float32)
    amplitudes = jnp.clip(jnp.exp(math.log(3.0) - 2.7080502 * jax.random.uniform(seeds[2], (ANGLES, TILES, PASSES, POS, FRAME, FRAME), jnp.float32) ** level_of(seeds[2], (ANGLES, TILES, PASSES, POS, FRAME, FRAME), ((0, 4), (1, 8)), -0.2, 0.2)), 0.2, 3.0)
    positions = draw_positions(jax.random.fold_in(seeds[4], 71), 0)
    return dict(object_field=object_field, probe=probe, amplitudes=amplitudes, positions=positions)


def dft_tables(size):
    index = jnp.arange(size, dtype=jnp.int32)
    product = index[:, None] * index[None, :] % size
    phase = product.astype(jnp.float32) * (2.0 * math.pi / size)
    scale = 1.0 / math.sqrt(size)
    return (jnp.cos(phase) * scale, -jnp.sin(phase) * scale)

def transform(xr, xi, ar, ai):
    high = lax.Precision.HIGHEST
    left_r = jnp.einsum('ab,pmbc->pmac', ar, xr, precision=high) - jnp.einsum('ab,pmbc->pmac', ai, xi, precision=high)
    left_i = jnp.einsum('ab,pmbc->pmac', ar, xi, precision=high) + jnp.einsum('ab,pmbc->pmac', ai, xr, precision=high)
    out_r = jnp.einsum('pmab,bc->pmac', left_r, ar, precision=high) - jnp.einsum('pmab,bc->pmac', left_i, ai, precision=high)
    out_i = jnp.einsum('pmab,bc->pmac', left_r, ai, precision=high) + jnp.einsum('pmab,bc->pmac', left_i, ar, precision=high)
    return (out_r, out_i)

def frame_work(patches, probe, amp):
    size = probe.shape[-1]
    table_r, table_i = dft_tables(size)
    probe_r, probe_i = (probe[0][None], probe[1][None])
    patch_r, patch_i = (patches[:, 0][:, None], patches[:, 1][:, None])
    exit_r = probe_r * patch_r - probe_i * patch_i
    exit_i = probe_r * patch_i + probe_i * patch_r
    wave_r, wave_i = transform(exit_r, exit_i, table_r, table_i)
    inten = lax.optimization_barrier(jnp.sum(wave_r * wave_r + wave_i * wave_i, axis=1, keepdims=True))
    factor = amp[:, None] / jnp.maximum(jnp.sqrt(inten), 0.5) - 1.0
    back_r, back_i = transform(wave_r * factor, wave_i * factor, table_r, -table_i)
    grad_r = lax.optimization_barrier(jnp.sum(probe_r * back_r + probe_i * back_i, axis=1))
    grad_i = lax.optimization_barrier(jnp.sum(probe_r * back_i - probe_i * back_r, axis=1))
    probe_gr = lax.optimization_barrier(jnp.sum(patch_r * back_r + patch_i * back_i, axis=0))
    probe_gi = lax.optimization_barrier(jnp.sum(patch_r * back_i - patch_i * back_r, axis=0))
    weight = lax.optimization_barrier(jnp.sum(patches[:, 0] ** 2 + patches[:, 1] ** 2, axis=0))
    return (grad_r, grad_i, probe_gr, probe_gi, weight)

def extract(extended, rows, cols, size):

    def one(row, col):
        zero = jnp.zeros((), jnp.int32)
        return lax.dynamic_slice(extended, (zero, row.astype(jnp.int32), col.astype(jnp.int32)), (extended.shape[0], size, size))
    return jax.vmap(one)(rows, cols)

def accumulate(buffer, values, rows, cols):
    size = values.shape[-1]

    def step(j, acc):
        zero = jnp.zeros((), jnp.int32)
        start = (zero, rows[j].astype(jnp.int32), cols[j].astype(jnp.int32))
        current = lax.dynamic_slice(acc, start, (acc.shape[0], size, size))
        return lax.dynamic_update_slice(acc, current + values[j], start)
    return lax.fori_loop(0, values.shape[0], step, buffer)

def reference(object_field, probe, amplitudes, positions):
    wframe = lax.optimization_barrier(jnp.sum(probe * probe, axis=(0, 1)))
    outs = []
    probe_grad = jnp.zeros_like(probe)
    probe_weight = jnp.zeros((FRAME, FRAME), jnp.float32)
    for angle in range(ANGLES):
        obj = object_field[angle]
        for step in range(PASSES):
            extended = jnp.pad(obj, ((0, 0), (HALF, HALF), (0, 0)))
            offsets = jnp.arange(TILES, dtype=jnp.int32) * ROWS

            def per_tile(inputs):
                pos, amp, offset = inputs
                rows = pos[:, 0] + offset
                patches = extract(extended, rows, pos[:, 1], FRAME)
                grad_r, grad_i, probe_gr, probe_gi, weight = frame_work(patches, probe, amp)
                lights = jnp.broadcast_to(wframe, grad_r.shape)
                return (jnp.stack([grad_r, grad_i, lights], axis=1), probe_gr, probe_gi, weight)
            values, probe_gr, probe_gi, weight = lax.map(per_tile, (positions[angle, :, step], amplitudes[angle, :, step], offsets))
            rows = (positions[angle, :, step, :, 0] + offsets[:, None]).reshape(-1)
            cols = positions[angle, :, step, :, 1].reshape(-1)
            buffer = jnp.zeros((3, OBJ_ROWS + 2 * HALF, WIDTH), jnp.float32)
            acc = accumulate(buffer, values.reshape((-1, 3, FRAME, FRAME)), rows, cols)[:, HALF:HALF + OBJ_ROWS]
            reg = 0.1 * jnp.sum(acc[2]) / (OBJ_ROWS * WIDTH)
            obj = obj + acc[:2] / (acc[2] + reg)
            if step == PASSES - 1:
                probe_grad = probe_grad + jnp.stack([lax.optimization_barrier(jnp.sum(probe_gr, axis=0)), lax.optimization_barrier(jnp.sum(probe_gi, axis=0))])
                probe_weight = probe_weight + lax.optimization_barrier(jnp.sum(weight, axis=0))
        outs.append(obj)
    probe_out = probe + probe_grad / (probe_weight + 0.1 * jnp.mean(probe_weight))
    return (jnp.stack(outs), probe_out)
```

```python
import functools
import math

import jax
import jax.numpy as jnp
import numpy as np
from jax import lax
from jax.experimental import pallas as pl
from jax.experimental.pallas import tpu as pltpu
from jax.sharding import PartitionSpec as P

F32 = jnp.float32
BF16 = jnp.bfloat16
MESH = pl.DeviceIdType.MESH


def dft_parts(size):
    index = np.arange(size)
    phase = (index[:, None] * index[None, :] % size) * (2.0 * math.pi / size)
    return np.stack([np.cos(phase), -np.sin(phase)]).astype(np.float64) / math.sqrt(size)


def split(value):
    high = value.astype(BF16)
    return high, (value - high.astype(F32)).astype(BF16)


def dot(a, b):
    return jnp.dot(a, b, preferred_element_type=F32)


def kernel(
    tiles, angles, pos, obj, probe, amp, dft, out_obj, out_probe,
    mats, field, place, wplace, acc, light, grecv, patch, wsum,
    postile, posrecv, npos, town, trecv, regs, qbuf, rbuf, qout,
    halo_s, halo_r, pos_s, pos_r, tot_s, tot_r, g_s, g_r, rs_s, rs_r, ag_s, ag_r, loc,
):
    t = lax.axis_index("tile")
    a = lax.axis_index("angle")
    passes, count = pos.shape[0], pos.shape[2]
    size = probe.shape[-1]
    half = size // 2
    strip = obj.shape[1]
    width = obj.shape[2]
    rows = strip + 2 * half
    has_above, has_below = t > 0, t < tiles - 1
    span = strip

    abits = [1 << b for b in range((angles - 1).bit_length())]
    tbits = [1 << b for b in range((tiles - 1).bit_length())]

    def xor(index, bit):
        return index + bit - 2 * bit * lax.rem(index // bit, 2)

    barrier = pltpu.get_barrier_semaphore()
    for d in range(1, tiles):
        pl.semaphore_signal(barrier, inc=1, device_id={"tile": lax.rem(t + d, tiles)}, device_id_type=MESH)
    for bit in abits:
        pl.semaphore_signal(barrier, inc=1, device_id={"angle": xor(a, bit)}, device_id_type=MESH)

    for c in range(2):
        for part, term in enumerate(split(dft[c])):
            for k in range(2):
                if c == 0:
                    mats[2 * k + part, 0:size, 0:size] = term
                    mats[2 * k + part, size : 2 * size, size : 2 * size] = term
                else:
                    mats[2 * k + part, 0:size, size : 2 * size] = -term if k else term
                    mats[2 * k + part, size : 2 * size, 0:size] = term if k else -term
    for h in range(2):
        field[:, h, half : half + strip] = obj[:, :, h * size : (h + 1) * size]

    @pl.when(t == 0)
    def _():
        field[:, :, 0:half] = jnp.zeros((2, 2, half, size), F32)
        posrecv[0] = jnp.zeros((8, 128), jnp.int32)
        grecv[:, 0] = jnp.zeros(grecv.shape[:1] + grecv.shape[2:], F32)

    @pl.when(t == tiles - 1)
    def _():
        field[:, :, rows - half : rows] = jnp.zeros((2, 2, half, size), F32)
        posrecv[1] = jnp.zeros((8, 128), jnp.int32)
        grecv[:, 1] = jnp.zeros(grecv.shape[:1] + grecv.shape[2:], F32)

    wframe = jnp.zeros((size, size), F32)
    for c in range(2):
        for m in range(2):
            wframe = wframe + probe[c, m] * probe[c, m]
    wsum[...] = wframe

    lane = lax.broadcasted_iota(jnp.int32, (8, 128), 1)
    ptile = jnp.zeros((8, 128), jnp.int32)
    for p in range(passes):
        for j in range(count):
            for k in range(2):
                ptile = jnp.where(lane == (p * count + j) * 2 + k, pos[p, k, j], ptile)
    postile[...] = ptile

    frow = lax.broadcasted_iota(jnp.int32, (size, size), 0)
    for p in range(passes):
        part = jnp.zeros((size, size), F32)
        for j in range(count):
            row = t * strip + pos[p, 0, j] - half + frow
            part = part + jnp.where((row >= 0) & (row < tiles * strip), wframe, 0.0)
        town[p] = jnp.sum(part.reshape(size // 8, 8, size), axis=0)

    def halo(d):
        if d == 0:
            return pltpu.make_async_remote_copy(
                src_ref=field.at[:, :, half : 2 * half], dst_ref=field.at[:, :, rows - half : rows],
                send_sem=halo_s.at[0], recv_sem=halo_r.at[0], device_id={"tile": t - 1}, device_id_type=MESH)
        return pltpu.make_async_remote_copy(
            src_ref=field.at[:, :, rows - 2 * half : rows - half], dst_ref=field.at[:, :, 0:half],
            send_sem=halo_s.at[1], recv_sem=halo_r.at[1], device_id={"tile": t + 1}, device_id_type=MESH)

    def posc(d):
        return pltpu.make_async_remote_copy(
            src_ref=postile, dst_ref=posrecv.at[1 - d],
            send_sem=pos_s.at[d], recv_sem=pos_r.at[d],
            device_id={"tile": t - 1 if d == 0 else t + 1}, device_id_type=MESH)

    def totc(d):
        return pltpu.make_async_remote_copy(
            src_ref=town, dst_ref=trecv.at[d], send_sem=tot_s.at[d], recv_sem=tot_r.at[d],
            device_id={"tile": lax.rem(t + d, tiles)}, device_id_type=MESH)

    def gradc(p, c, d, last):
        if d == 0:
            src = acc.at[p, c, :, 0:half] if last else acc.at[p, c, :, 0:size]
            dst = grecv.at[p, 1, c, :, 0:half] if last else grecv.at[p, 1, c]
        else:
            src = acc.at[p, c, :, rows - half : rows] if last else acc.at[p, c, :, rows - size : rows]
            dst = grecv.at[p, 0, c, :, half:size] if last else grecv.at[p, 0, c]
        return pltpu.make_async_remote_copy(
            src_ref=src, dst_ref=dst, send_sem=g_s.at[p, c, d], recv_sem=g_r.at[p, c, d],
            device_id={"tile": t - 1 if d == 0 else t + 1}, device_id_type=MESH)

    sends = ((0, has_above), (1, has_below))
    arrivals = ((0, has_below), (1, has_above))

    pl.semaphore_wait(barrier, tiles - 1 + len(abits))

    for d, ok in sends:
        @pl.when(ok)
        def _(d=d):
            halo(d).start()
    for d, ok in sends:
        @pl.when(ok)
        def _(d=d):
            posc(d).start()
    for d in range(1, tiles):
        totc(d).start()

    for buf in (place, wplace):
        flat = buf.shape[:-2]
        for index in np.ndindex(*flat):
            buf[index + (slice(0, span),)] = jnp.zeros((span, size), F32)
            buf[index + (slice(span + size, 2 * span + size),)] = jnp.zeros((span, size), F32)

    for d, ok in arrivals:
        @pl.when(ok)
        def _(d=d):
            halo(d).wait_recv()

    flane = lax.broadcasted_iota(jnp.int32, (size, size), 1)

    def put(buf, index, value, col):
        rolled = pltpu.roll(value, lax.rem(col, size), 1)
        buf[index + (0, slice(span, span + size))] = jnp.where(flane >= col, rolled, 0.0)
        buf[index + (1, slice(span, span + size))] = jnp.where(flane < col, rolled, 0.0)

    def mul(k, value, left):
        high, low = split(value)
        mh, ml = mats[2 * k], mats[2 * k + 1]
        if left:
            return dot(mh, high) + (dot(ml, high) + dot(mh, low))
        return dot(high, mh) + (dot(high, ml) + dot(low, mh))

    def swap(v):
        top = jnp.concatenate([v[:size, :size], v[size:, :size]], axis=1)
        low = jnp.concatenate([v[:size, size:], v[size:, size:]], axis=1)
        return jnp.concatenate([top, low], axis=0)

    def do_pass(p, last):
        at = [(pos[p, 0, j], pos[p, 1, j]) for j in range(count)]
        for j, (r, c) in enumerate(at):
            shift = lax.rem(size - c, size)
            for k in range(2):
                one = pltpu.roll(field[k, 0, pl.ds(r, size)], shift, 1)
                two = pltpu.roll(field[k, 1, pl.ds(r, size)], shift, 1)
                patch[j, k] = jnp.where(flane < size - c, one, two)
        waves = []
        for j in range(count):
            pr, pi = patch[j, 0], patch[j, 1]
            re = [probe[0, m] * pr - probe[1, m] * pi for m in range(2)]
            im = [probe[0, m] * pi + probe[1, m] * pr for m in range(2)]
            x = jnp.concatenate([jnp.concatenate(re, axis=1), jnp.concatenate(im, axis=1)], axis=0)
            waves.append(mul(1, x, True))
        waves = [mul(0, swap(v), False) for v in waves]
        backs = []
        for j, v in enumerate(waves):
            sq = v * v
            inten = sq[:size, :size] + sq[:size, size:] + sq[size:, :size] + sq[size:, size:]
            factor = amp[p, j] * lax.rsqrt(jnp.maximum(inten, 0.25)) - 1.0
            factor = jnp.concatenate([factor, factor], axis=1)
            backs.append(mul(1, v * jnp.concatenate([factor, factor], axis=0), False))
        chis = [mul(0, swap(v), True) for v in backs]

        def chi(j, c, m):
            return chis[j][c * size : (c + 1) * size, m * size : (m + 1) * size]

        if last:
            for m in range(2):
                qr = jnp.zeros((size, size), F32)
                qi = jnp.zeros((size, size), F32)
                for j in range(count):
                    pr, pi = patch[j, 0], patch[j, 1]
                    qr = qr + (pr * chi(j, 0, m) + pi * chi(j, 1, m))
                    qi = qi + (pr * chi(j, 1, m) - pi * chi(j, 0, m))
                qbuf[m * size : (m + 1) * size] = qr
                qbuf[(2 + m) * size : (3 + m) * size] = qi
            v = jnp.zeros((size, size), F32)
            for j in range(count):
                v = v + patch[j, 0] * patch[j, 0] + patch[j, 1] * patch[j, 1]
            qbuf[4 * size : 5 * size] = v
            rs_start(0)

        for c in range(2):
            for j in range(count):
                if c == 0:
                    g = sum(probe[0, m] * chi(j, 0, m) + probe[1, m] * chi(j, 1, m) for m in range(2))
                else:
                    g = sum(probe[0, m] * chi(j, 1, m) - probe[1, m] * chi(j, 0, m) for m in range(2))
                put(place, (j, c), g, at[j][1])
            for h in range(2):
                total = place[0, c, h, pl.ds(span - at[0][0], rows)]
                for j in range(1, count):
                    total = total + place[j, c, h, pl.ds(span - at[j][0], rows)]
                acc[p, c, h] = total
            for d, ok in sends:
                @pl.when(ok)
                def _(d=d, c=c):
                    gradc(p, c, d, last).start()

        @pl.when(p == 0)
        def _():
            for d, ok in sends:
                @pl.when(ok)
                def _(d=d):
                    halo(d).wait_send()
            for d, ok in arrivals:
                @pl.when(ok)
                def _(d=d):
                    posc(d).wait_recv()
            copy = pltpu.make_async_copy(posrecv, npos, loc)
            copy.start()
            copy.wait()
            totals = town[...]
            for d in range(1, tiles):
                totc(d).wait_recv()
                totals = totals + trecv[d]
            for q in range(passes):
                regs[q] = jnp.sum(totals[q]) * (0.1 / (strip * tiles * width))

        w = wsum[...]
        for j in range(count):
            put(wplace, (j,), w, at[j][1])
            for n in range(2):
                put(wplace, (count * (1 + n) + j,), w, npos[n, 0, (p * count + j) * 2 + 1])
        for h in range(2):
            total = wplace[0, h, pl.ds(span - at[0][0], rows)]
            for j in range(1, count):
                total = total + wplace[j, h, pl.ds(span - at[j][0], rows)]
            light[h] = total
            for n, ok in ((0, has_above), (1, has_below)):
                base = 2 * span if n == 0 else span
                zone = jnp.zeros((size, size), F32)
                for j in range(count):
                    start = base - npos[n, 0, (p * count + j) * 2]
                    zone = zone + wplace[count * (1 + n) + j, h, pl.ds(start, size)]
                spot = slice(0, size) if n == 0 else slice(rows - size, rows)
                light[h, spot] = light[h, spot] + jnp.where(ok, zone, 0.0)
        reg = regs[p]

        def update(lo, hi, recv, ok, outside):
            for h in range(2):
                den = light[h, lo:hi] + reg
                for c in range(2):
                    g = acc[p, c, h, lo:hi]
                    if recv is not None:
                        g = g + grecv[p, recv[0], c, h, recv[1]]
                    new = field[c, h, lo:hi] + g / den
                    if last:
                        out_obj[c, lo - half : hi - half, h * size : (h + 1) * size] = new
                    else:
                        if outside is not None:
                            row = lax.broadcasted_iota(jnp.int32, new.shape, 0)
                            inside = (row >= half) if outside == 0 else (row < size - half)
                            new = jnp.where(inside | ok, new, 0.0)
                        field[c, h, lo:hi] = new

        update(size, rows - size, None, None, None)
        for d, ok in arrivals:
            @pl.when(ok)
            def _(d=d):
                for c in range(2):
                    gradc(p, c, d, last).wait_recv()
        if last:
            update(half, size, (0, slice(half, size)), has_above, None)
            update(rows - size, rows - half, (1, slice(0, half)), has_below, None)
        else:
            update(0, size, (0, slice(0, size)), has_above, 0)
            update(rows - size, rows, (1, slice(0, size)), has_below, 1)

    steps = []
    n = qbuf.shape[0]
    off = 0
    for axis, index, bits in (("tile", t, tbits), ("angle", a, abits)):
        for bit in bits:
            other = xor(index, bit)
            halved = (n // 2) % 8 == 0
            if halved:
                n //= 2
                side = lax.rem(index // bit, 2)
                keep, send = off + side * n, off + (1 - side) * n
            else:
                keep = send = off
            steps.append((axis, other, n, halved, keep, send))
            off = keep

    def piece(start, length):
        return pl.ds(pl.multiple_of(start, 8), length)

    def rs_copy(s):
        axis, other, n, _, _, send = steps[s]
        return pltpu.make_async_remote_copy(
            src_ref=qbuf.at[piece(send, n)], dst_ref=rbuf.at[s, 0:n],
            send_sem=rs_s.at[s], recv_sem=rs_r.at[s], device_id={axis: other}, device_id_type=MESH)

    def rs_start(s):
        rs_copy(s).start()

    def ag_copy(s):
        axis, other, n, _, keep, _ = steps[s]
        return pltpu.make_async_remote_copy(
            src_ref=qout.at[piece(keep, n)], dst_ref=qout.at[piece(keep, n)],
            send_sem=ag_s.at[s], recv_sem=ag_r.at[s], device_id={axis: other}, device_id_type=MESH)

    def ag_arrival(s):
        axis, other, n, _, _, send = steps[s]
        return pltpu.make_async_remote_copy(
            src_ref=qout.at[piece(send, n)], dst_ref=qout.at[piece(send, n)],
            send_sem=ag_s.at[s], recv_sem=ag_r.at[s], device_id={axis: other}, device_id_type=MESH)

    def step(p, carry):
        do_pass(p, False)
        return carry

    lax.fori_loop(0, passes - 1, step, 0)
    do_pass(passes - 1, True)

    for s, (axis, other, n, halved, keep, send) in enumerate(steps):
        if s > 0:
            rs_start(s)
        rs_copy(s).wait()
        spot = piece(keep, n)
        mine = qbuf[spot] + rbuf[s, 0:n]
        if s == len(steps) - 1:
            qout[spot] = mine
        else:
            qbuf[spot] = mine
    for s in reversed(range(len(steps))):
        if steps[s][3]:
            ag_copy(s).start()
            ag_copy(s).wait_send()
            ag_arrival(s).wait_recv()

    v = qout[4 * size : 5 * size]
    den = v + jnp.sum(v) * (0.1 / (size * size))
    for c in range(2):
        for m in range(2):
            k = 2 * c + m
            out_probe[c, m] = probe[c, m] + qout[k * size : (k + 1) * size] / den

    for d, ok in sends:
        @pl.when(ok)
        def _(d=d):
            posc(d).wait_send()
            for p in range(passes):
                for c in range(2):
                    gradc(p, c, d, p == passes - 1).wait_send()
    for d in range(1, tiles):
        totc(d).wait_send()


def body(tiles, angles, object_field, probe, amplitudes, positions):
    obj, amp, pos = object_field[0], amplitudes[0, 0], positions[0, 0]
    pos = jnp.swapaxes(pos, 1, 2)
    passes, count = pos.shape[0], pos.shape[2]
    size = probe.shape[-1]
    strip = obj.shape[1]
    rows = strip + size
    deep = 2 * strip + size
    stages = (tiles - 1).bit_length() + (angles - 1).bit_length()
    vm = pltpu.VMEM
    dma = pltpu.SemaphoreType.DMA
    scratch = [
        vm((4, 2 * size, 2 * size), BF16),
        vm((2, 2, rows, size), F32),
        vm((count, 2, 2, deep, size), F32),
        vm((3 * count, 2, deep, size), F32),
        vm((passes, 2, 2, rows, size), F32),
        vm((2, rows, size), F32),
        vm((passes, 2, 2, 2, size, size), F32),
        vm((count, 2, size, size), F32),
        vm((size, size), F32),
        vm((8, 128), jnp.int32),
        vm((2, 8, 128), jnp.int32),
        pltpu.SMEM((2, 8, 128), jnp.int32),
        vm((passes, 8, size), F32),
        vm((tiles, passes, 8, size), F32),
        pltpu.SMEM((passes,), F32),
        vm((5 * size, size), F32),
        vm((stages, 5 * size // 2, size), F32),
        vm((5 * size, size), F32),
        dma((2,)), dma((2,)), dma((2,)), dma((2,)),
        dma((tiles,)), dma((tiles,)),
        dma((passes, 2, 2)), dma((passes, 2, 2)),
        dma((stages,)), dma((stages,)), dma((stages,)), dma((stages,)),
        dma,
    ]
    vmem = pl.BlockSpec(memory_space=pltpu.VMEM)
    out_obj, out_probe = pl.pallas_call(
        functools.partial(kernel, tiles, angles),
        out_shape=(jax.ShapeDtypeStruct(obj.shape, F32), jax.ShapeDtypeStruct(probe.shape, F32)),
        in_specs=[pl.BlockSpec(memory_space=pltpu.SMEM), vmem, vmem, vmem, vmem],
        out_specs=(vmem, vmem),
        scratch_shapes=scratch,
        compiler_params=pltpu.CompilerParams(
            collective_id=0, has_side_effects=True, vmem_limit_bytes=50 * 1024 * 1024
        ),
    )(pos, obj, probe, amp, jnp.asarray(dft_parts(size), F32))
    return out_obj[None], out_probe


def solution(mesh):
    tiles, angles = mesh.shape["tile"], mesh.shape["angle"]
    return jax.shard_map(
        functools.partial(body, tiles, angles),
        mesh=mesh,
        in_specs=(
            P("angle", None, "tile", None),
            P(),
            P("angle", "tile", None, None, None, None),
            P("angle", "tile", None, None, None),
        ),
        out_specs=(P("angle", None, "tile", None), P()),
        check_vma=False,
    )
```

```python
import functools
import math

import jax
import jax.numpy as jnp
import numpy as np
from jax import lax
from jax.experimental import pallas as pl
from jax.experimental.pallas import tpu as pltpu
from jax.sharding import PartitionSpec as P

F32 = jnp.float32
BF16 = jnp.bfloat16
MESH = pl.DeviceIdType.MESH


def dft_parts(size):
    index = np.arange(size)
    phase = (index[:, None] * index[None, :] % size) * (2.0 * math.pi / size)
    return np.stack([np.cos(phase), -np.sin(phase)]).astype(np.float64) / math.sqrt(size)


def split(value):
    high = value.astype(BF16)
    return high, (value - high.astype(F32)).astype(BF16)


def dot(a, b):
    return jnp.dot(a, b, preferred_element_type=F32)


def groups(tiles, angles):
    out = []
    bits = (tiles - 1).bit_length()
    shift = 0
    while shift < bits:
        take = 1 if shift == 0 else min(2, bits - shift)
        out.append(("tile", shift, 1 << take))
        shift += take
    bits = (angles - 1).bit_length()
    shift = 0
    while shift < bits:
        take = min(2, bits - shift)
        out.append(("angle", shift, 1 << take))
        shift += take
    return out


def plan(tiles, angles, size):
    chunks, base, sem = [], 0, 0
    for start, length in ((0, size), (size, 2 * size), (3 * size, 2 * size)):
        phases, n = [], length
        for axis, shift, members in groups(tiles, angles):
            cut = n % (8 * members) == 0
            n = n // members if cut else n
            phases.append((axis, shift, members, cut, n, base, sem))
            base += members * n
            sem += members - 1
        chunks.append((start, length, phases))
    return chunks, base, sem


def kernel(
    tiles, angles, pos_in, obj_in, probe_in, amp_in, dft_in, out_obj, out_probe,
    pos, probe, amp, dft,
    mats, field, place, wplace, acc, light, grecv, patch, wsum,
    postile, posrecv, npos, town, trecv, regs, qbuf, rbuf, qout,
    halo_s, halo_r, pos_s, pos_r, tot_s, tot_r, g_s, g_r, rs_s, rs_r, ag_s, ag_r, loc, in_s,
):
    t = lax.axis_index("tile")
    a = lax.axis_index("angle")
    passes, count = pos_in.shape[0], pos_in.shape[2]
    size = probe_in.shape[-1]
    half = size // 2
    strip = obj_in.shape[1]
    width = obj_in.shape[2]
    rows = strip + 2 * half
    has_above, has_below = t > 0, t < tiles - 1
    span = strip

    def load(k, src, dst):
        return pltpu.make_async_copy(src, dst, in_s.at[k])

    loads = [
        load(0, pos_in, pos), load(1, probe_in, probe), load(2, dft_in, dft),
        load(3, obj_in.at[:, :, 0:size], field.at[:, 0, half : half + strip]),
        load(4, obj_in.at[:, :, size : 2 * size], field.at[:, 1, half : half + strip]),
        load(5, amp_in, amp),
    ]
    for copy in loads:
        copy.start()

    barrier = pltpu.get_barrier_semaphore()
    for d in range(1, tiles):
        pl.semaphore_signal(barrier, inc=1, device_id={"tile": lax.rem(t + d, tiles)}, device_id_type=MESH)
    for d in range(1, angles):
        pl.semaphore_signal(barrier, inc=1, device_id={"angle": lax.rem(a + d, angles)}, device_id_type=MESH)

    @pl.when(t == 0)
    def _():
        field[:, :, 0:half] = jnp.zeros((2, 2, half, size), F32)
        posrecv[0] = jnp.zeros((8, 128), jnp.int32)
        grecv[:, 0] = jnp.zeros(grecv.shape[:1] + grecv.shape[2:], F32)

    @pl.when(t == tiles - 1)
    def _():
        field[:, :, rows - half : rows] = jnp.zeros((2, 2, half, size), F32)
        posrecv[1] = jnp.zeros((8, 128), jnp.int32)
        grecv[:, 1] = jnp.zeros(grecv.shape[:1] + grecv.shape[2:], F32)

    def halo(d, h):
        cols = slice(h * size, (h + 1) * size)
        if d == 0:
            src, dst = obj_in.at[:, 0:half, cols], field.at[:, h, rows - half : rows]
        else:
            src, dst = obj_in.at[:, strip - half : strip, cols], field.at[:, h, 0:half]
        return pltpu.make_async_remote_copy(
            src_ref=src, dst_ref=dst, send_sem=halo_s.at[d, h], recv_sem=halo_r.at[d, h],
            device_id={"tile": t - 1 if d == 0 else t + 1}, device_id_type=MESH)

    def posc(d):
        return pltpu.make_async_remote_copy(
            src_ref=postile, dst_ref=posrecv.at[1 - d],
            send_sem=pos_s.at[d], recv_sem=pos_r.at[d],
            device_id={"tile": t - 1 if d == 0 else t + 1}, device_id_type=MESH)

    def totc(d):
        return pltpu.make_async_remote_copy(
            src_ref=town, dst_ref=trecv.at[d], send_sem=tot_s.at[d], recv_sem=tot_r.at[d],
            device_id={"tile": lax.rem(t + d, tiles)}, device_id_type=MESH)

    def gradc(p, c, d, last):
        if d == 0:
            src = acc.at[p, c, :, 0:half] if last else acc.at[p, c, :, 0:size]
            dst = grecv.at[p, 1, c, :, 0:half] if last else grecv.at[p, 1, c]
        else:
            src = acc.at[p, c, :, rows - half : rows] if last else acc.at[p, c, :, rows - size : rows]
            dst = grecv.at[p, 0, c, :, half:size] if last else grecv.at[p, 0, c]
        return pltpu.make_async_remote_copy(
            src_ref=src, dst_ref=dst, send_sem=g_s.at[p, c, d], recv_sem=g_r.at[p, c, d],
            device_id={"tile": t - 1 if d == 0 else t + 1}, device_id_type=MESH)

    sends = ((0, has_above), (1, has_below))
    arrivals = ((0, has_below), (1, has_above))

    for buf in (place, wplace):
        flat = buf.shape[:-2]
        for index in np.ndindex(*flat):
            buf[index + (slice(0, span),)] = jnp.zeros((span, size), F32)
            buf[index + (slice(span + size, 2 * span + size),)] = jnp.zeros((span, size), F32)

    pl.semaphore_wait(barrier, tiles - 1 + angles - 1)

    for d, ok in sends:
        @pl.when(ok)
        def _(d=d):
            for h in range(2):
                halo(d, h).start()

    loads[0].wait()
    loads[1].wait()
    wframe = jnp.zeros((size, size), F32)
    for c in range(2):
        for m in range(2):
            wframe = wframe + probe[c, m] * probe[c, m]
    wsum[...] = wframe

    lane = lax.broadcasted_iota(jnp.int32, (8, 128), 1)
    ptile = jnp.zeros((8, 128), jnp.int32)
    for p in range(passes):
        for j in range(count):
            for k in range(2):
                ptile = jnp.where(lane == (p * count + j) * 2 + k, pos[p, k, j], ptile)
    postile[...] = ptile

    frow = lax.broadcasted_iota(jnp.int32, (size, size), 0)
    for p in range(passes):
        part = jnp.zeros((size, size), F32)
        for j in range(count):
            row = t * strip + pos[p, 0, j] - half + frow
            part = part + jnp.where((row >= 0) & (row < tiles * strip), wframe, 0.0)
        town[p] = jnp.sum(part.reshape(size // 8, 8, size), axis=0)

    for d, ok in sends:
        @pl.when(ok)
        def _(d=d):
            posc(d).start()
    for d in range(1, tiles):
        totc(d).start()

    loads[2].wait()
    for c in range(2):
        for part, term in enumerate(split(dft[c])):
            for k in range(2):
                if c == 0:
                    mats[2 * k + part, 0:size, 0:size] = term
                    mats[2 * k + part, size : 2 * size, size : 2 * size] = term
                else:
                    mats[2 * k + part, 0:size, size : 2 * size] = -term if k else term
                    mats[2 * k + part, size : 2 * size, 0:size] = term if k else -term

    loads[3].wait()
    loads[4].wait()
    for d, ok in arrivals:
        @pl.when(ok)
        def _(d=d):
            for h in range(2):
                halo(d, h).wait_recv()

    loads[5].wait()

    flane = lax.broadcasted_iota(jnp.int32, (size, size), 1)

    def put(buf, index, value, col):
        rolled = pltpu.roll(value, lax.rem(col, size), 1)
        buf[index + (0, slice(span, span + size))] = jnp.where(flane >= col, rolled, 0.0)
        buf[index + (1, slice(span, span + size))] = jnp.where(flane < col, rolled, 0.0)

    def mul(k, value, left):
        high, low = split(value)
        mh, ml = mats[2 * k], mats[2 * k + 1]
        if left:
            return dot(mh, high) + (dot(ml, high) + dot(mh, low))
        return dot(high, mh) + (dot(high, ml) + dot(low, mh))

    def swap(v):
        top = jnp.concatenate([v[:size, :size], v[size:, :size]], axis=1)
        low = jnp.concatenate([v[:size, size:], v[size:, size:]], axis=1)
        return jnp.concatenate([top, low], axis=0)

    def do_pass(p, last):
        at = [(pos[p, 0, j], pos[p, 1, j]) for j in range(count)]
        for j, (r, c) in enumerate(at):
            shift = lax.rem(size - c, size)
            for k in range(2):
                one = pltpu.roll(field[k, 0, pl.ds(r, size)], shift, 1)
                two = pltpu.roll(field[k, 1, pl.ds(r, size)], shift, 1)
                patch[j, k] = jnp.where(flane < size - c, one, two)
        if last:
            v = jnp.zeros((size, size), F32)
            for j in range(count):
                v = v + patch[j, 0] * patch[j, 0] + patch[j, 1] * patch[j, 1]
            qbuf[0:size] = v
            advance(0)
        waves = []
        for j in range(count):
            pr, pi = patch[j, 0], patch[j, 1]
            re = [probe[0, m] * pr - probe[1, m] * pi for m in range(2)]
            im = [probe[0, m] * pi + probe[1, m] * pr for m in range(2)]
            x = jnp.concatenate([jnp.concatenate(re, axis=1), jnp.concatenate(im, axis=1)], axis=0)
            waves.append(mul(1, x, True))
        if last:
            advance(0)
        waves = [mul(0, swap(v), False) for v in waves]
        if last:
            advance(0)
        backs = []
        for j, v in enumerate(waves):
            sq = v * v
            inten = sq[:size, :size] + sq[:size, size:] + sq[size:, :size] + sq[size:, size:]
            factor = amp[p, j] * lax.rsqrt(jnp.maximum(inten, 0.25)) - 1.0
            factor = jnp.concatenate([factor, factor], axis=1)
            backs.append(mul(1, v * jnp.concatenate([factor, factor], axis=0), False))
        if last:
            advance(0)
        chis = [mul(0, swap(v), True) for v in backs]

        def chi(j, c, m):
            return chis[j][c * size : (c + 1) * size, m * size : (m + 1) * size]

        if last:
            for m in range(2):
                qr = jnp.zeros((size, size), F32)
                qi = jnp.zeros((size, size), F32)
                for j in range(count):
                    pr, pi = patch[j, 0], patch[j, 1]
                    qr = qr + (pr * chi(j, 0, m) + pi * chi(j, 1, m))
                    qi = qi + (pr * chi(j, 1, m) - pi * chi(j, 0, m))
                qbuf[(1 + 2 * m) * size : (2 + 2 * m) * size] = qr
                qbuf[(2 + 2 * m) * size : (3 + 2 * m) * size] = qi
                advance(1 + m)
            advance(0)

        for c in range(2):
            for j in range(count):
                if c == 0:
                    g = sum(probe[0, m] * chi(j, 0, m) + probe[1, m] * chi(j, 1, m) for m in range(2))
                else:
                    g = sum(probe[0, m] * chi(j, 1, m) - probe[1, m] * chi(j, 0, m) for m in range(2))
                put(place, (j, c), g, at[j][1])
            for h in range(2):
                total = place[0, c, h, pl.ds(span - at[0][0], rows)]
                for j in range(1, count):
                    total = total + place[j, c, h, pl.ds(span - at[j][0], rows)]
                acc[p, c, h] = total
            for d, ok in sends:
                @pl.when(ok)
                def _(d=d, c=c):
                    gradc(p, c, d, last).start()
            if last:
                advance(1, 2)

        @pl.when(p == 0)
        def _():
            for d, ok in arrivals:
                @pl.when(ok)
                def _(d=d):
                    posc(d).wait_recv()
            copy = pltpu.make_async_copy(posrecv, npos, loc)
            copy.start()
            copy.wait()
            totals = town[...]
            for d in range(1, tiles):
                totc(d).wait_recv()
                totals = totals + trecv[d]
            for q in range(passes):
                regs[q] = jnp.sum(totals[q]) * (0.1 / (strip * tiles * width))

        w = wsum[...]
        for j in range(count):
            put(wplace, (j,), w, at[j][1])
            for n in range(2):
                put(wplace, (count * (1 + n) + j,), w, npos[n, 0, (p * count + j) * 2 + 1])
        for h in range(2):
            total = wplace[0, h, pl.ds(span - at[0][0], rows)]
            for j in range(1, count):
                total = total + wplace[j, h, pl.ds(span - at[j][0], rows)]
            light[h] = total
            for n, ok in ((0, has_above), (1, has_below)):
                base = 2 * span if n == 0 else span
                zone = jnp.zeros((size, size), F32)
                for j in range(count):
                    start = base - npos[n, 0, (p * count + j) * 2]
                    zone = zone + wplace[count * (1 + n) + j, h, pl.ds(start, size)]
                spot = slice(0, size) if n == 0 else slice(rows - size, rows)
                light[h, spot] = light[h, spot] + jnp.where(ok, zone, 0.0)
        reg = regs[p]

        def update(lo, hi, recv, ok, outside):
            for h in range(2):
                den = light[h, lo:hi] + reg
                for c in range(2):
                    g = acc[p, c, h, lo:hi]
                    if recv is not None:
                        g = g + grecv[p, recv[0], c, h, recv[1]]
                    new = field[c, h, lo:hi] + g / den
                    if last:
                        out_obj[c, lo - half : hi - half, h * size : (h + 1) * size] = new
                    else:
                        if outside is not None:
                            row = lax.broadcasted_iota(jnp.int32, new.shape, 0)
                            inside = (row >= half) if outside == 0 else (row < size - half)
                            new = jnp.where(inside | ok, new, 0.0)
                        field[c, h, lo:hi] = new

        if last:
            advance(1, 2)
        update(size, rows - size, None, None, None)
        if last:
            advance(1, 2)
        for d, ok in arrivals:
            @pl.when(ok)
            def _(d=d):
                for c in range(2):
                    gradc(p, c, d, last).wait_recv()
        if last:
            update(half, size, (0, slice(half, size)), has_above, None)
            update(rows - size, rows - half, (1, slice(0, half)), has_below, None)
        else:
            update(0, size, (0, slice(0, size)), has_above, 0)
            update(rows - size, rows, (1, slice(0, size)), has_below, 1)

    chunks, _, _ = plan(tiles, angles, size)
    index_of = {"tile": t, "angle": a}

    def piece(start, length):
        return pl.ds(pl.multiple_of(start, 8), length)

    def member(k, f):
        axis, shift, members = chunks[k][2][f][:3]
        return lax.rem(index_of[axis] // (1 << shift), members)

    def parent(k, f):
        start = chunks[k][0]
        for e in range(f):
            if chunks[k][2][e][3]:
                start = start + member(k, e) * chunks[k][2][e][4]
        return start

    def peer(k, f, d):
        axis, shift, members = chunks[k][2][f][:3]
        i = member(k, f)
        other = lax.rem(i + d, members)
        return other, {axis: index_of[axis] + (other - i) * (1 << shift)}

    def spot(k, f, i):
        _, _, _, cut, n, _, _ = chunks[k][2][f]
        return piece(parent(k, f) + (i * n if cut else 0), n)

    def rs_copy(k, f, d, arrival=False):
        _, _, members, _, n, base, sem = chunks[k][2][f]
        i = member(k, f)
        other, device = peer(k, f, d)
        slot = lax.rem(i + members - d, members) if arrival else i
        return pltpu.make_async_remote_copy(
            src_ref=qbuf.at[spot(k, f, other)], dst_ref=rbuf.at[piece(base + slot * n, n)],
            send_sem=rs_s.at[sem + d - 1], recv_sem=rs_r.at[sem + d - 1],
            device_id=device, device_id_type=MESH)

    def ag_copy(k, f, d, arrival=False):
        _, _, members, _, _, _, sem = chunks[k][2][f]
        i = member(k, f)
        _, device = peer(k, f, d)
        from_i = lax.rem(i + members - d, members) if arrival else i
        where = spot(k, f, from_i)
        return pltpu.make_async_remote_copy(
            src_ref=qout.at[where], dst_ref=qout.at[where],
            send_sem=ag_s.at[sem + d - 1], recv_sem=ag_r.at[sem + d - 1],
            device_id=device, device_id_type=MESH)

    count_f = len(chunks[0][2])

    def others(k, f):
        return range(1, chunks[k][2][f][2])

    def rs_start(k, f):
        _, _, _, _, n, base, _ = chunks[k][2][f]
        for d in others(k, f):
            rs_copy(k, f, d).start()
        i = member(k, f)
        rbuf[piece(base + i * n, n)] = qbuf[spot(k, f, i)]

    def rs_end(k, f):
        _, _, members, cut, n, base, _ = chunks[k][2][f]
        for d in others(k, f):
            rs_copy(k, f, d, True).wait_recv()
        total = rbuf[base : base + n]
        for m in range(1, members):
            total = total + rbuf[base + m * n : base + (m + 1) * n]
        i = member(k, f)
        if f == count_f - 1:
            qout[spot(k, f, i)] = total
        else:
            if not cut:
                for d in others(k, f):
                    rs_copy(k, f, d).wait_send()
            qbuf[spot(k, f, i)] = total

    def cuts(k):
        return [f for f in reversed(range(count_f)) if chunks[k][2][f][3]]

    def ag_start(k, f):
        for d in others(k, f):
            ag_copy(k, f, d).start()

    def ag_end(k, f):
        for d in others(k, f):
            ag_copy(k, f, d, True).wait_recv()

    def script(k):
        ends = []
        for f in range(count_f):
            yield (ends.pop() if ends else None, functools.partial(rs_start, k, f))
            ends.append(functools.partial(rs_end, k, f))
        for f in cuts(k):
            yield (ends.pop(), functools.partial(ag_start, k, f))
            ends.append(functools.partial(ag_end, k, f))
        yield (ends.pop(), None)

    scripts = [script(k) for k in range(3)]

    def advance(*which):
        moved = False
        for k in which:
            for end, start in [next(scripts[k], (None, None))]:
                if end is not None:
                    end()
                if start is not None:
                    start()
                moved = moved or end is not None or start is not None
        return moved

    def step(p, carry):
        do_pass(p, False)
        return carry

    lax.fori_loop(0, passes - 1, step, 0)
    do_pass(passes - 1, True)

    while advance(0, 1, 2):
        pass

    v = qout[0:size]
    den = v + jnp.sum(v) * (0.1 / (size * size))
    for c in range(2):
        for m in range(2):
            k = 1 + 2 * m + c
            out_probe[c, m] = probe[c, m] + qout[k * size : (k + 1) * size] / den

    for d, ok in sends:
        @pl.when(ok)
        def _(d=d):
            posc(d).wait_send()
            for h in range(2):
                halo(d, h).wait_send()
            for p in range(passes):
                for c in range(2):
                    gradc(p, c, d, p == passes - 1).wait_send()
    for d in range(1, tiles):
        totc(d).wait_send()
    for k in range(3):
        for f in range(count_f):
            for d in others(k, f):
                if chunks[k][2][f][3] or f == count_f - 1:
                    rs_copy(k, f, d).wait_send()
                if chunks[k][2][f][3]:
                    ag_copy(k, f, d).wait_send()


def body(tiles, angles, object_field, probe, amplitudes, positions):
    obj, amp, pos = object_field[0], amplitudes[0, 0], positions[0, 0]
    pos = jnp.swapaxes(pos, 1, 2)
    passes, count = pos.shape[0], pos.shape[2]
    size = probe.shape[-1]
    strip = obj.shape[1]
    rows = strip + size
    deep = 2 * strip + size
    _, slots, copies = plan(tiles, angles, size)
    vm = pltpu.VMEM
    dma = pltpu.SemaphoreType.DMA
    scratch = [
        pltpu.SMEM(pos.shape, jnp.int32),
        vm(probe.shape, F32),
        vm(amp.shape, F32),
        vm((2, size, size), F32),
        vm((4, 2 * size, 2 * size), BF16),
        vm((2, 2, rows, size), F32),
        vm((count, 2, 2, deep, size), F32),
        vm((3 * count, 2, deep, size), F32),
        vm((passes, 2, 2, rows, size), F32),
        vm((2, rows, size), F32),
        vm((passes, 2, 2, 2, size, size), F32),
        vm((count, 2, size, size), F32),
        vm((size, size), F32),
        vm((8, 128), jnp.int32),
        vm((2, 8, 128), jnp.int32),
        pltpu.SMEM((2, 8, 128), jnp.int32),
        vm((passes, 8, size), F32),
        vm((tiles, passes, 8, size), F32),
        pltpu.SMEM((passes,), F32),
        vm((5 * size, size), F32),
        vm((slots, size), F32),
        vm((5 * size, size), F32),
        dma((2, 2)), dma((2, 2)), dma((2,)), dma((2,)),
        dma((tiles,)), dma((tiles,)),
        dma((passes, 2, 2)), dma((passes, 2, 2)),
        dma((copies,)), dma((copies,)), dma((copies,)), dma((copies,)),
        dma, dma((6,)),
    ]
    vmem = pl.BlockSpec(memory_space=pltpu.VMEM)
    out_obj, out_probe = pl.pallas_call(
        functools.partial(kernel, tiles, angles),
        out_shape=(jax.ShapeDtypeStruct(obj.shape, F32), jax.ShapeDtypeStruct(probe.shape, F32)),
        in_specs=[pl.BlockSpec(memory_space=pltpu.HBM)] * 5,
        out_specs=(vmem, vmem),
        scratch_shapes=scratch,
        compiler_params=pltpu.CompilerParams(
            collective_id=0, has_side_effects=True, vmem_limit_bytes=60 * 1024 * 1024
        ),
    )(pos, obj, probe, amp, jnp.asarray(dft_parts(size), F32))
    return out_obj[None], out_probe


def solution(mesh):
    tiles, angles = mesh.shape["tile"], mesh.shape["angle"]
    return jax.shard_map(
        functools.partial(body, tiles, angles),
        mesh=mesh,
        in_specs=(
            P("angle", None, "tile", None),
            P(),
            P("angle", "tile", None, None, None, None),
            P("angle", "tile", None, None, None),
        ),
        out_specs=(P("angle", None, "tile", None), P()),
        check_vma=False,
    )
```

```python
import functools
import math

import jax
import jax.numpy as jnp
import numpy as np
from jax import lax
from jax.experimental import pallas as pl
from jax.experimental.pallas import tpu as pltpu
from jax.sharding import PartitionSpec as P

F32 = jnp.float32
BF16 = jnp.bfloat16
MESH = pl.DeviceIdType.MESH


def dft_parts(size):
    index = np.arange(size)
    phase = (index[:, None] * index[None, :] % size) * (2.0 * math.pi / size)
    return np.stack([np.cos(phase), -np.sin(phase)]).astype(np.float64) / math.sqrt(size)


def split(value):
    high = value.astype(BF16)
    return high, (value - high.astype(F32)).astype(BF16)


def dot(a, b):
    return jnp.dot(a, b, preferred_element_type=F32)


def groups(tiles, angles):
    out = []
    bits = (tiles - 1).bit_length()
    shift = 0
    while shift < bits:
        take = 1 if shift == 0 else min(2, bits - shift)
        out.append(("tile", shift, 1 << take))
        shift += take
    bits = (angles - 1).bit_length()
    shift = 0
    while shift < bits:
        take = min(2, bits - shift)
        out.append(("angle", shift, 1 << take))
        shift += take
    return out


def plan(tiles, angles, size):
    chunks, base, sem = [], 0, 0
    for start, length in ((0, 5 * size),):
        phases, n = [], length
        for axis, shift, members in groups(tiles, angles):
            cut = n % (8 * members) == 0
            n = n // members if cut else n
            phases.append((axis, shift, members, cut, n, base, sem))
            base += members * n
            sem += members - 1
        chunks.append((start, length, phases))
    return chunks, base, sem


def kernel(
    tiles, angles, pos_in, obj_in, probe_in, amp_in, dft_in, out_obj, out_probe,
    done, pos, probe, amp, dft,
    mats, field, place, wplace, acc, light, grecv, patch, wsum,
    postile, posrecv, npos, town, trecv, regs, qbuf, rbuf, qout,
    halo_s, halo_r, pos_s, pos_r, tot_s, tot_r, g_s, g_r, rs_s, rs_r, ag_s, ag_r, loc, in_s,
):
    t = lax.axis_index("tile")
    a = lax.axis_index("angle")
    passes, count = pos_in.shape[0], pos_in.shape[2]
    size = probe_in.shape[-1]
    half = size // 2
    strip = obj_in.shape[1]
    width = obj_in.shape[2]
    rows = strip + 2 * half
    has_above, has_below = t > 0, t < tiles - 1
    span = strip

    def load(k, src, dst):
        return pltpu.make_async_copy(src, dst, in_s.at[k])

    loads = [
        load(0, pos_in, pos), load(1, probe_in, probe), load(2, dft_in, dft),
        load(3, obj_in.at[:, :, 0:size], field.at[:, 0, half : half + strip]),
        load(4, obj_in.at[:, :, size : 2 * size], field.at[:, 1, half : half + strip]),
        load(5, amp_in, amp),
    ]
    for copy in loads:
        copy.start()

    barrier = pltpu.get_barrier_semaphore()
    for d in range(1, tiles):
        pl.semaphore_signal(barrier, inc=1, device_id={"tile": lax.rem(t + d, tiles)}, device_id_type=MESH)
    for d in range(1, angles):
        pl.semaphore_signal(barrier, inc=1, device_id={"angle": lax.rem(a + d, angles)}, device_id_type=MESH)

    @pl.when(t == 0)
    def _():
        field[:, :, 0:half] = jnp.zeros((2, 2, half, size), F32)
        posrecv[0] = jnp.zeros((8, 128), jnp.int32)
        grecv[:, 0] = jnp.zeros(grecv.shape[:1] + grecv.shape[2:], F32)

    @pl.when(t == tiles - 1)
    def _():
        field[:, :, rows - half : rows] = jnp.zeros((2, 2, half, size), F32)
        posrecv[1] = jnp.zeros((8, 128), jnp.int32)
        grecv[:, 1] = jnp.zeros(grecv.shape[:1] + grecv.shape[2:], F32)

    def halo(d, h):
        cols = slice(h * size, (h + 1) * size)
        if d == 0:
            src, dst = obj_in.at[:, 0:half, cols], field.at[:, h, rows - half : rows]
        else:
            src, dst = obj_in.at[:, strip - half : strip, cols], field.at[:, h, 0:half]
        return pltpu.make_async_remote_copy(
            src_ref=src, dst_ref=dst, send_sem=halo_s.at[d, h], recv_sem=halo_r.at[d, h],
            device_id={"tile": t - 1 if d == 0 else t + 1}, device_id_type=MESH)

    def posc(d):
        return pltpu.make_async_remote_copy(
            src_ref=postile, dst_ref=posrecv.at[1 - d],
            send_sem=pos_s.at[d], recv_sem=pos_r.at[d],
            device_id={"tile": t - 1 if d == 0 else t + 1}, device_id_type=MESH)

    def totc(end, d):
        return pltpu.make_async_remote_copy(
            src_ref=town, dst_ref=trecv.at[end], send_sem=tot_s.at[d], recv_sem=tot_r.at[end],
            device_id={"tile": lax.rem(t + d, tiles)}, device_id_type=MESH)

    def gradc(p, d, last):
        if d == 0:
            src = acc.at[p, :, :, 0:half] if last else acc.at[p, :, :, 0:size]
            dst = grecv.at[p, 1, :, :, 0:half] if last else grecv.at[p, 1]
        else:
            src = acc.at[p, :, :, rows - half : rows] if last else acc.at[p, :, :, rows - size : rows]
            dst = grecv.at[p, 0, :, :, half:size] if last else grecv.at[p, 0]
        return pltpu.make_async_remote_copy(
            src_ref=src, dst_ref=dst, send_sem=g_s.at[p, d], recv_sem=g_r.at[p, d],
            device_id={"tile": t - 1 if d == 0 else t + 1}, device_id_type=MESH)

    sends = ((0, has_above), (1, has_below))
    arrivals = ((0, has_below), (1, has_above))
    for buf in (place, wplace):
        flat = buf.shape[:-2]
        for index in np.ndindex(*flat):
            buf[index + (slice(0, span),)] = jnp.zeros((span, size), F32)
            buf[index + (slice(span + size, 2 * span + size),)] = jnp.zeros((span, size), F32)

    pl.semaphore_wait(barrier, tiles - 1 + angles - 1)

    for d, ok in sends:
        @pl.when(ok)
        def _(d=d):
            for h in range(2):
                halo(d, h).start()

    loads[0].wait()
    loads[1].wait()
    wframe = jnp.zeros((size, size), F32)
    for c in range(2):
        for m in range(2):
            wframe = wframe + probe[c, m] * probe[c, m]
    wsum[...] = wframe

    lane = lax.broadcasted_iota(jnp.int32, (8, 128), 1)
    ptile = jnp.zeros((8, 128), jnp.int32)
    for p in range(passes):
        for j in range(count):
            for k in range(2):
                ptile = jnp.where(lane == (p * count + j) * 2 + k, pos[p, k, j], ptile)
    postile[...] = ptile

    frow = lax.broadcasted_iota(jnp.int32, (size, size), 0)
    for p in range(passes):
        part = jnp.zeros((size, size), F32)
        for j in range(count):
            row = t * strip + pos[p, 0, j] - half + frow
            part = part + jnp.where((row >= 0) & (row < tiles * strip), wframe, 0.0)
        town[p] = jnp.sum(part.reshape(size // 8, 8, size), axis=0)

    for d, ok in sends:
        @pl.when(ok)
        def _(d=d):
            posc(d).start()
    for end, mine in ((0, t == 0), (1, t == tiles - 1)):
        @pl.when(mine)
        def _(end=end):
            for d in range(1, tiles):
                totc(end, d).start()
            trecv[end] = town[...]

    loads[2].wait()
    for c in range(2):
        for part, term in enumerate(split(dft[c])):
            for k in range(2):
                if c == 0:
                    mats[2 * k + part, 0:size, 0:size] = term
                    mats[2 * k + part, size : 2 * size, size : 2 * size] = term
                else:
                    mats[2 * k + part, 0:size, size : 2 * size] = -term if k else term
                    mats[2 * k + part, size : 2 * size, 0:size] = term if k else -term

    loads[3].wait()
    loads[4].wait()
    for d, ok in arrivals:
        @pl.when(ok)
        def _(d=d):
            for h in range(2):
                halo(d, h).wait_recv()

    loads[5].wait()

    flane = lax.broadcasted_iota(jnp.int32, (size, size), 1)

    def put(buf, index, value, col):
        rolled = pltpu.roll(value, lax.rem(col, size), 1)
        buf[index + (0, slice(span, span + size))] = jnp.where(flane >= col, rolled, 0.0)
        buf[index + (1, slice(span, span + size))] = jnp.where(flane < col, rolled, 0.0)

    def mul(k, value, left):
        high, low = split(value)
        mh, ml = mats[2 * k], mats[2 * k + 1]
        if left:
            return dot(mh, high) + (dot(ml, high) + dot(mh, low))
        return dot(high, mh) + (dot(high, ml) + dot(low, mh))

    def swap(v):
        top = jnp.concatenate([v[:size, :size], v[size:, :size]], axis=1)
        low = jnp.concatenate([v[:size, size:], v[size:, size:]], axis=1)
        return jnp.concatenate([top, low], axis=0)

    def do_pass(p, last):
        at = [(pos[p, 0, j], pos[p, 1, j]) for j in range(count)]
        for j, (r, c) in enumerate(at):
            shift = lax.rem(size - c, size)
            for k in range(2):
                one = pltpu.roll(field[k, 0, pl.ds(r, size)], shift, 1)
                two = pltpu.roll(field[k, 1, pl.ds(r, size)], shift, 1)
                patch[j, k] = jnp.where(flane < size - c, one, two)
        if last:
            v = jnp.zeros((size, size), F32)
            for j in range(count):
                v = v + patch[j, 0] * patch[j, 0] + patch[j, 1] * patch[j, 1]
            qbuf[0:size] = v
        waves = []
        for j in range(count):
            pr, pi = patch[j, 0], patch[j, 1]
            re = [probe[0, m] * pr - probe[1, m] * pi for m in range(2)]
            im = [probe[0, m] * pi + probe[1, m] * pr for m in range(2)]
            x = jnp.concatenate([jnp.concatenate(re, axis=1), jnp.concatenate(im, axis=1)], axis=0)
            waves.append(mul(1, x, True))
        waves = [mul(0, swap(v), False) for v in waves]
        backs = []
        for j, v in enumerate(waves):
            sq = v * v
            inten = sq[:size, :size] + sq[:size, size:] + sq[size:, :size] + sq[size:, size:]
            factor = amp[p, j] * lax.rsqrt(jnp.maximum(inten, 0.25)) - 1.0
            factor = jnp.concatenate([factor, factor], axis=1)
            backs.append(mul(1, v * jnp.concatenate([factor, factor], axis=0), False))
        chis = [mul(0, swap(v), True) for v in backs]

        def chi(j, c, m):
            return chis[j][c * size : (c + 1) * size, m * size : (m + 1) * size]

        if last:
            for m in range(2):
                qr = jnp.zeros((size, size), F32)
                qi = jnp.zeros((size, size), F32)
                for j in range(count):
                    pr, pi = patch[j, 0], patch[j, 1]
                    qr = qr + (pr * chi(j, 0, m) + pi * chi(j, 1, m))
                    qi = qi + (pr * chi(j, 1, m) - pi * chi(j, 0, m))
                qbuf[(1 + 2 * m) * size : (2 + 2 * m) * size] = qr
                qbuf[(2 + 2 * m) * size : (3 + 2 * m) * size] = qi
            advance(0)

        for c in range(2):
            for j in range(count):
                if c == 0:
                    g = sum(probe[0, m] * chi(j, 0, m) + probe[1, m] * chi(j, 1, m) for m in range(2))
                else:
                    g = sum(probe[0, m] * chi(j, 1, m) - probe[1, m] * chi(j, 0, m) for m in range(2))
                put(place, (j, c), g, at[j][1])
            for h in range(2):
                total = place[0, c, h, pl.ds(span - at[0][0], rows)]
                for j in range(1, count):
                    total = total + place[j, c, h, pl.ds(span - at[j][0], rows)]
                acc[p, c, h] = total
            if last and c == 0:
                advance(0)
        for d, ok in sends:
            @pl.when(ok)
            def _(d=d):
                gradc(p, d, last).start()

        @pl.when(p == 0)
        def _():
            for d, ok in arrivals:
                @pl.when(ok)
                def _(d=d):
                    posc(d).wait_recv()
            copy = pltpu.make_async_copy(posrecv, npos, loc)
            copy.start()
            copy.wait()
            for end, other in ((0, t != 0), (1, t != tiles - 1)):
                @pl.when(other)
                def _(end=end):
                    totc(end, 1).wait_recv()
            within = jnp.sum(wsum[...].reshape(size // 8, 8, size), axis=0)
            totals = trecv[0] + trecv[1] + within * float((tiles - 2) * count)
            for q in range(passes):
                regs[q] = jnp.sum(totals[q]) * (0.1 / (strip * tiles * width))

        w = wsum[...]
        for j in range(count):
            put(wplace, (j,), w, at[j][1])
            for n in range(2):
                put(wplace, (count * (1 + n) + j,), w, npos[n, 0, (p * count + j) * 2 + 1])
        for h in range(2):
            total = wplace[0, h, pl.ds(span - at[0][0], rows)]
            for j in range(1, count):
                total = total + wplace[j, h, pl.ds(span - at[j][0], rows)]
            light[h] = total
            for n, ok in ((0, has_above), (1, has_below)):
                base = 2 * span if n == 0 else span
                zone = jnp.zeros((size, size), F32)
                for j in range(count):
                    start = base - npos[n, 0, (p * count + j) * 2]
                    zone = zone + wplace[count * (1 + n) + j, h, pl.ds(start, size)]
                spot = slice(0, size) if n == 0 else slice(rows - size, rows)
                light[h, spot] = light[h, spot] + jnp.where(ok, zone, 0.0)
        reg = regs[p]

        def update(lo, hi, recv, ok, outside):
            for h in range(2):
                den = light[h, lo:hi] + reg
                for c in range(2):
                    g = acc[p, c, h, lo:hi]
                    if recv is not None:
                        g = g + grecv[p, recv[0], c, h, recv[1]]
                    new = field[c, h, lo:hi] + g / den
                    if last:
                        done[c, lo - half : hi - half, h * size : (h + 1) * size] = new
                    else:
                        if outside is not None:
                            row = lax.broadcasted_iota(jnp.int32, new.shape, 0)
                            inside = (row >= half) if outside == 0 else (row < size - half)
                            new = jnp.where(inside | ok, new, 0.0)
                        field[c, h, lo:hi] = new

        update(size, rows - size, None, None, None)
        if last:
            advance(0)
        for d, ok in arrivals:
            @pl.when(ok)
            def _(d=d):
                gradc(p, d, last).wait_recv()
        if last:
            update(half, size, (0, slice(half, size)), has_above, None)
            update(rows - size, rows - half, (1, slice(0, half)), has_below, None)
        else:
            update(0, size, (0, slice(0, size)), has_above, 0)
            update(rows - size, rows, (1, slice(0, size)), has_below, 1)

    chunks, _, _ = plan(tiles, angles, size)
    index_of = {"tile": t, "angle": a}

    def piece(start, length):
        return pl.ds(pl.multiple_of(start, 8), length)

    def member(k, f):
        axis, shift, members = chunks[k][2][f][:3]
        return lax.rem(index_of[axis] // (1 << shift), members)

    def parent(k, f):
        start = chunks[k][0]
        for e in range(f):
            if chunks[k][2][e][3]:
                start = start + member(k, e) * chunks[k][2][e][4]
        return start

    def peer(k, f, d):
        axis, shift, members = chunks[k][2][f][:3]
        i = member(k, f)
        other = lax.rem(i + d, members)
        return other, {axis: index_of[axis] + (other - i) * (1 << shift)}

    def spot(k, f, i):
        _, _, _, cut, n, _, _ = chunks[k][2][f]
        return piece(parent(k, f) + (i * n if cut else 0), n)

    def rs_copy(k, f, d, arrival=False):
        _, _, members, _, n, base, sem = chunks[k][2][f]
        i = member(k, f)
        other, device = peer(k, f, d)
        slot = lax.rem(i + members - d, members) if arrival else i
        return pltpu.make_async_remote_copy(
            src_ref=qbuf.at[spot(k, f, other)], dst_ref=rbuf.at[piece(base + slot * n, n)],
            send_sem=rs_s.at[sem + d - 1], recv_sem=rs_r.at[sem + d - 1],
            device_id=device, device_id_type=MESH)

    def ag_copy(k, f, d, arrival=False):
        _, _, members, _, _, _, sem = chunks[k][2][f]
        i = member(k, f)
        _, device = peer(k, f, d)
        from_i = lax.rem(i + members - d, members) if arrival else i
        where = spot(k, f, from_i)
        return pltpu.make_async_remote_copy(
            src_ref=qout.at[where], dst_ref=qout.at[where],
            send_sem=ag_s.at[sem + d - 1], recv_sem=ag_r.at[sem + d - 1],
            device_id=device, device_id_type=MESH)

    count_f = len(chunks[0][2])

    def others(k, f):
        return range(1, chunks[k][2][f][2])

    def rs_start(k, f):
        _, _, _, _, n, base, _ = chunks[k][2][f]
        for d in others(k, f):
            rs_copy(k, f, d).start()
        i = member(k, f)
        rbuf[piece(base + i * n, n)] = qbuf[spot(k, f, i)]

    def rs_end(k, f):
        _, _, members, cut, n, base, _ = chunks[k][2][f]
        for d in others(k, f):
            rs_copy(k, f, d, True).wait_recv()
        total = rbuf[base : base + n]
        for m in range(1, members):
            total = total + rbuf[base + m * n : base + (m + 1) * n]
        i = member(k, f)
        if f == count_f - 1:
            qout[spot(k, f, i)] = total
        else:
            if not cut:
                for d in others(k, f):
                    rs_copy(k, f, d).wait_send()
            qbuf[spot(k, f, i)] = total

    def cuts(k):
        return [f for f in reversed(range(count_f)) if chunks[k][2][f][3]]

    def ag_start(k, f):
        for d in others(k, f):
            ag_copy(k, f, d).start()

    def ag_end(k, f):
        for d in others(k, f):
            ag_copy(k, f, d, True).wait_recv()

    def script(k):
        ends = []
        for f in range(count_f):
            yield (ends.pop() if ends else None, functools.partial(rs_start, k, f))
            ends.append(functools.partial(rs_end, k, f))
        for f in cuts(k):
            yield (ends.pop(), functools.partial(ag_start, k, f))
            ends.append(functools.partial(ag_end, k, f))
        yield (ends.pop(), None)

    scripts = [script(k) for k in range(1)]

    def advance(*which):
        moved = False
        for k in which:
            for end, start in [next(scripts[k], (None, None))]:
                if end is not None:
                    end()
                if start is not None:
                    start()
                moved = moved or end is not None or start is not None
        return moved

    def step(p, carry):
        do_pass(p, False)
        return carry

    lax.fori_loop(0, passes - 1, step, 0)
    do_pass(passes - 1, True)

    leave = pltpu.make_async_copy(done, out_obj, loc)
    leave.start()
    while advance(0):
        pass

    v = qout[0:size]
    den = v + jnp.sum(v) * (0.1 / (size * size))
    for c in range(2):
        for m in range(2):
            k = 1 + 2 * m + c
            out_probe[c, m] = probe[c, m] + qout[k * size : (k + 1) * size] / den

    for d, ok in sends:
        @pl.when(ok)
        def _(d=d):
            posc(d).wait_send()
            for h in range(2):
                halo(d, h).wait_send()
            for p in range(passes):
                gradc(p, d, p == passes - 1).wait_send()
    leave.wait()
    for end, mine in ((0, t == 0), (1, t == tiles - 1)):
        @pl.when(mine)
        def _(end=end):
            for d in range(1, tiles):
                totc(end, d).wait_send()
    for k in range(1):
        for f in range(count_f):
            for d in others(k, f):
                if chunks[k][2][f][3] or f == count_f - 1:
                    rs_copy(k, f, d).wait_send()
                if chunks[k][2][f][3]:
                    ag_copy(k, f, d).wait_send()


def body(tiles, angles, object_field, probe, amplitudes, positions):
    obj, amp, pos = object_field[0], amplitudes[0, 0], positions[0, 0]
    pos = jnp.swapaxes(pos, 1, 2)
    passes, count = pos.shape[0], pos.shape[2]
    size = probe.shape[-1]
    strip = obj.shape[1]
    rows = strip + size
    deep = 2 * strip + size
    _, slots, copies = plan(tiles, angles, size)
    vm = pltpu.VMEM
    dma = pltpu.SemaphoreType.DMA
    scratch = [
        vm(obj.shape, F32),
        pltpu.SMEM(pos.shape, jnp.int32),
        vm(probe.shape, F32),
        vm(amp.shape, F32),
        vm((2, size, size), F32),
        vm((4, 2 * size, 2 * size), BF16),
        vm((2, 2, rows, size), F32),
        vm((count, 2, 2, deep, size), F32),
        vm((3 * count, 2, deep, size), F32),
        vm((passes, 2, 2, rows, size), F32),
        vm((2, rows, size), F32),
        vm((passes, 2, 2, 2, size, size), F32),
        vm((count, 2, size, size), F32),
        vm((size, size), F32),
        vm((8, 128), jnp.int32),
        vm((2, 8, 128), jnp.int32),
        pltpu.SMEM((2, 8, 128), jnp.int32),
        vm((passes, 8, size), F32),
        vm((2, passes, 8, size), F32),
        pltpu.SMEM((passes,), F32),
        vm((5 * size, size), F32),
        vm((slots, size), F32),
        vm((5 * size, size), F32),
        dma((2, 2)), dma((2, 2)), dma((2,)), dma((2,)),
        dma((tiles,)), dma((2,)),
        dma((passes, 2)), dma((passes, 2)),
        dma((copies,)), dma((copies,)), dma((copies,)), dma((copies,)),
        dma, dma((6,)),
    ]
    vmem = pl.BlockSpec(memory_space=pltpu.VMEM)
    out_obj, out_probe = pl.pallas_call(
        functools.partial(kernel, tiles, angles),
        out_shape=(jax.ShapeDtypeStruct(obj.shape, F32), jax.ShapeDtypeStruct(probe.shape, F32)),
        in_specs=[pl.BlockSpec(memory_space=pltpu.HBM)] * 5,
        out_specs=(pl.BlockSpec(memory_space=pltpu.HBM), vmem),
        scratch_shapes=scratch,
        compiler_params=pltpu.CompilerParams(
            collective_id=0, has_side_effects=True, vmem_limit_bytes=60 * 1024 * 1024
        ),
    )(pos, obj, probe, amp, jnp.asarray(dft_parts(size), F32))
    return out_obj[None], out_probe


def solution(mesh):
    tiles, angles = mesh.shape["tile"], mesh.shape["angle"]
    return jax.shard_map(
        functools.partial(body, tiles, angles),
        mesh=mesh,
        in_specs=(
            P("angle", None, "tile", None),
            P(),
            P("angle", "tile", None, None, None, None),
            P("angle", "tile", None, None, None),
        ),
        out_specs=(P("angle", None, "tile", None), P()),
        check_vma=False,
    )
```
